32 devices in a mesh: dp: 8 (over z, x), seq: 4 (over y, core).
Axes of the slice: x: 2, y: 2, z: 4, core: 2. Of those that a mesh axis runs over, the one named last changes fastest.
Arguments:
- encoder_input: bfloat16 [128, 64, 768], P(('dp', 'seq')), may hold values from -6 to 6
- visible_patches: int32 [128, 64], P(('dp', 'seq')), may hold values from 0 to 255, as said below
- sensor_index: int32 [128], P(('dp', 'seq')), may hold values from 0 to 3
- encoder_gain: bfloat16 [768], P(('dp', 'seq')), may hold values from 0.5 to 1.5
- encoder_attend: bfloat16 [768, 2304], P(('dp', 'seq')), may hold values from -0.21875 to 0.21875
- encoder_merge: bfloat16 [768, 768], P(('dp', 'seq')), may hold values from -0.625 to 0.625
- encoder_midnorm: bfloat16 [768], P(('dp', 'seq')), may hold values from 0.5 to 1.5
- encoder_expand: bfloat16 [768, 3072], P(('dp', 'seq')), may hold values from -0.21875 to 0.21875
- encoder_reduce: bfloat16 [3072, 768], P(('dp', 'seq')), may hold values from -0.109375 to 0.109375
- narrowing: bfloat16 [768, 512], P(('dp', 'seq')), may hold values from -0.21875 to 0.21875
- placeholder: bfloat16 [4, 512], P(None, ('dp', 'seq')), may hold values from -6 to 6
- decoder_gain: bfloat16 [512], P(('dp', 'seq')), may hold values from 0.5 to 1.5
- decoder_attend: bfloat16 [512, 768], P(('dp', 'seq')), may hold values from -0.25 to 0.25
- decoder_merge: bfloat16 [256, 512], P(('dp', 'seq')), may hold values from -1.5 to 1.5
- decoder_midnorm: bfloat16 [512], P(('dp', 'seq')), may hold values from 0.5 to 1.5
- decoder_expand: bfloat16 [512, 2048], P(('dp', 'seq')), may hold values from -0.25 to 0.25
- decoder_reduce: bfloat16 [2048, 512], P(('dp', 'seq')), may hold values from -0.125 to 0.125
- cotangent: bfloat16 [128, 256, 512], P(('dp', 'seq')), may hold values from -6 to 6
Outputs:
- decoded: bfloat16 [128, 256, 512], P(('dp', 'seq'))
- input_gradient: bfloat16 [128, 64, 768], P(('dp', 'seq'))
- encoder_gain_gradient: float32 [768], P(('dp', 'seq'))
- encoder_attend_gradient: float32 [768, 2304], P(('dp', 'seq'))
- encoder_merge_gradient: float32 [768, 768], P(('dp', 'seq'))
- encoder_midnorm_gradient: float32 [768], P(('dp', 'seq'))
- encoder_expand_gradient: float32 [768, 3072], P(('dp', 'seq'))
- encoder_reduce_gradient: float32 [3072, 768], P(('dp', 'seq'))
- narrowing_gradient: float32 [768, 512], P(('dp', 'seq'))
- placeholder_gradient: float32 [4, 512], P(None, ('dp', 'seq'))
- decoder_gain_gradient: float32 [512], P(('dp', 'seq'))
- decoder_attend_gradient: float32 [512, 768], P(('dp', 'seq'))
- decoder_merge_gradient: float32 [256, 512], P(('dp', 'seq'))
- decoder_midnorm_gradient: float32 [512], P(('dp', 'seq'))
- decoder_expand_gradient: float32 [512, 2048], P(('dp', 'seq'))
- decoder_reduce_gradient: float32 [2048, 512], P(('dp', 'seq'))
The draws below stay inside these ranges and needn't reach their ends.
Inputs may be any that keep to these rules, and one draw needn't show every extreme that they name: `visible_patches`: each row holds 64 distinct patch numbers in rising order.
All inputs are finite; a program needn't handle non-finite values.
Results may differ from the reference program's by a relative error of at most 0.023.
Values may be sent and summed in bfloat16 or wider, within the bound.
A program may use at most 256 MiB of HBM per device.

```python
import math
import jax
import jax.numpy as jnp
from jax import lax

DE = 768
HD = 64
FE = 3072
DD = 512
HDD = 4
FD = 2048
PATCH = 256
VIS = 64
SENS = 4
CHIPS = 128


def draw_visible_patches(key, part):
    key = jax.random.fold_in(key, 11)
    chip_keys = jax.random.split(key, CHIPS)

    def choose(chip_key):
        shuffled = jax.random.permutation(chip_key, PATCH)
        return jnp.sort(shuffled[:VIS]).astype(jnp.int32)
    return jax.vmap(choose)(chip_keys)


def touch_ends(drawn, stream_key, low, largest):
    longest = drawn.shape.index(max(drawn.shape))
    spots = []
    for shift in (0, 1):
        where = [jax.random.randint(jax.random.fold_in(stream_key, axis), (), 0, length) for axis, length in enumerate(drawn.shape)]
        where[longest] = (where[longest] + shift) % drawn.shape[longest]
        spots.append(tuple(where))
    return drawn.at[spots[0]].set(low).at[spots[1]].set(largest)


def block_scale(key, dims, cuts, smallest, largest):
    level, own = 1.0, jax.random.fold_in(key, 6)
    for dim, blocks in cuts:
        steps = jnp.exp(jax.random.uniform(jax.random.fold_in(own, dim), (blocks,), jnp.float32, smallest / len(cuts), largest / len(cuts)))
        level = level * jnp.repeat(steps, dims[dim] // blocks).reshape([-1 if axis == dim else 1 for axis in range(len(dims))])
    return level


def scatter_about(stream_key, extent, width, bound, cuts=(), kind=jnp.bfloat16):
    factor_of = block_scale(stream_key, extent, cuts, -0.22, 0.18) if cuts else 1.0
    values = jax.random.normal(stream_key, extent, jnp.float32) * width * factor_of
    return jnp.minimum(jnp.maximum(values, -bound), bound).astype(kind)


def setup_inputs(seed: int = 0) -> dict:
    keys = jax.random.split(jax.random.key(seed), 19)
    return {
        "encoder_input": scatter_about(keys[0], (CHIPS, VIS, DE), 1.0, 6.0, ((0, 32),)),
        "visible_patches": draw_visible_patches(jax.random.fold_in(keys[18], 71), 0),
        "sensor_index": touch_ends(jax.random.randint(keys[2], (CHIPS,), 0, SENS), jax.random.fold_in(keys[2], 1), 0, SENS - 1).astype(jnp.int32),
        "encoder_gain": jnp.clip(1.0 + 0.1 * jax.random.normal(keys[3], (DE,), jnp.float32), 0.5, 1.5).astype(jnp.bfloat16),
        "encoder_attend": scatter_about(keys[4], (DE, 3 * DE), DE ** -0.5, 0.21875, ((0, 32),)),
        "encoder_merge": scatter_about(keys[5], (DE, DE), (DE // 8) ** -0.5, 0.625, ((0, 32),)),
        "encoder_midnorm": jnp.clip(1.0 + 0.1 * jax.random.normal(keys[6], (DE,), jnp.float32), 0.5, 1.5).astype(jnp.bfloat16),
        "encoder_expand": scatter_about(keys[7], (DE, FE), DE ** -0.5, 0.21875, ((0, 32),)),
        "encoder_reduce": scatter_about(keys[8], (FE, DE), FE ** -0.5, 0.109375, ((0, 32),)),
        "narrowing": scatter_about(keys[9], (DE, DD), DE ** -0.5, 0.21875, ((0, 32),)),
        "placeholder": scatter_about(keys[10], (SENS, DD), 1.0, 6.0, ((1, 32),)),
        "decoder_gain": jnp.clip(1.0 + 0.1 * jax.random.normal(keys[11], (DD,), jnp.float32), 0.5, 1.5).astype(jnp.bfloat16),
        "decoder_attend": scatter_about(keys[12], (DD, 3 * HDD * HD), DD ** -0.5, 0.25, ((0, 32),)),
        "decoder_merge": scatter_about(keys[13], (HDD * HD, DD), (HDD * HD // 16) ** -0.5, 1.5, ((0, 32),)),
        "decoder_midnorm": jnp.clip(1.0 + 0.1 * jax.random.normal(keys[14], (DD,), jnp.float32), 0.5, 1.5).astype(jnp.bfloat16),
        "decoder_expand": scatter_about(keys[15], (DD, FD), DD ** -0.5, 0.25, ((0, 32),)),
        "decoder_reduce": scatter_about(keys[16], (FD, DD), FD ** -0.5, 0.125, ((0, 32),)),
        "cotangent": scatter_about(keys[17], (CHIPS, PATCH, DD), 1.0, 6.0, ((0, 32),)),
    }


@jax.custom_vjp
def low(v):
    return lax.optimization_barrier(v.astype(jnp.bfloat16)).astype(jnp.float32)

@jax.custom_vjp
def low_back(v):
    return v

def low_keep(v):
    return (low(v), None)

def low_pass(kept, grad):
    return (grad,)

def back_keep(v):
    return (v, None)

def back_low(kept, grad):
    return (low(grad),)
low.defvjp(low_keep, low_pass)
low_back.defvjp(back_keep, back_low)
epsilon = 1e-05
highest = lax.Precision.HIGHEST

def product(left_side, right_side):
    return jnp.einsum('...i,ij->...j', left_side, right_side, precision=highest)

def layer_norm(stream, scale_gain):
    average = lax.optimization_barrier(jnp.mean(stream, axis=-1, keepdims=True))
    centred = stream - average
    return centred * lax.rsqrt(lax.optimization_barrier(jnp.mean(centred * centred, axis=-1, keepdims=True)) + epsilon) * scale_gain

def positions(patch_count, model_width):
    half_width = model_width // 2
    places = jnp.arange(patch_count, dtype=jnp.float32)[:, None]
    frequency = jnp.exp(jnp.arange(half_width, dtype=jnp.float32) * (-math.log(10000.0) / half_width))
    angles = places * frequency[None, :]
    return jnp.concatenate([jnp.sin(angles), jnp.cos(angles)], axis=1)

def block(stream, gain_first, attend_matrix, merge_matrix, gain_second, expand_matrix, reduce_matrix):
    chip_count, length, model_width = stream.shape
    head_count = attend_matrix.shape[1] // (3 * HD)
    normed = low(layer_norm(stream, gain_first))
    packed = low(low_back(product(normed, attend_matrix))).reshape(chip_count, length, 3, head_count, HD)
    queries, key_set, values = (packed[:, :, 0], packed[:, :, 1], packed[:, :, 2])
    scores = low_back(jnp.einsum('cqhd,ckhd->chqk', queries, key_set, precision=highest) * (1.0 / math.sqrt(HD)))
    soft_weights = low(jax.nn.softmax(scores, axis=-1))
    mixture = low(low_back(jnp.einsum('chqk,ckhd->cqhd', soft_weights, values, precision=highest)))
    mixture = mixture.reshape(chip_count, length, head_count * HD)
    middle = stream + low_back(product(mixture, merge_matrix))
    normed_two = low(layer_norm(middle, gain_second))
    hidden = low(jax.nn.gelu(low_back(product(normed_two, expand_matrix))))
    return middle + low_back(product(hidden, reduce_matrix))

def forward(token_rows, placing, sensor_onehot, weights):
    encoded = block(token_rows, weights[0], weights[1], weights[2], weights[3], weights[4], weights[5])
    narrowed = low(product(low(encoded), weights[6]))
    placed = jnp.einsum('cpv,cvj->cpj', placing, narrowed, precision=highest)
    absent = 1.0 - lax.optimization_barrier(jnp.sum(placing, axis=2))
    filler = product(sensor_onehot, weights[7])
    placed = placed + absent[:, :, None] * filler[:, None, :] + positions(PATCH, DD)[None]
    placed = low(low_back(placed))
    return block(placed, weights[8], weights[9], weights[10], weights[11], weights[12], weights[13])

def reference(encoder_input, visible_patches, sensor_index, encoder_gain, encoder_attend, encoder_merge, encoder_midnorm, encoder_expand, encoder_reduce, narrowing, placeholder, decoder_gain, decoder_attend, decoder_merge, decoder_midnorm, decoder_expand, decoder_reduce, cotangent):
    weights = tuple((matrix.astype(jnp.float32) for matrix in (encoder_gain, encoder_attend, encoder_merge, encoder_midnorm, encoder_expand, encoder_reduce, narrowing, placeholder, decoder_gain, decoder_attend, decoder_merge, decoder_midnorm, decoder_expand, decoder_reduce)))
    block_chips = math.gcd(CHIPS, 16)
    block_count = CHIPS // block_chips
    patch_numbers = jnp.arange(PATCH, dtype=jnp.int32)
    sensor_numbers = jnp.arange(SENS, dtype=jnp.int32)

    def advance(totals, pieces):
        token_rows, visible_rows, sensor_rows, cotangent_rows = pieces
        placing = (visible_rows[:, None, :] == patch_numbers[None, :, None]).astype(jnp.float32)
        sensor_onehot = (sensor_rows[:, None] == sensor_numbers[None, :]).astype(jnp.float32)

        def forward_run(stream, matrices):
            return forward(stream, placing, sensor_onehot, matrices)
        result, pullback = jax.vjp(forward_run, token_rows.astype(jnp.float32), weights)
        input_rows, weight_rows = pullback(cotangent_rows.astype(jnp.float32))
        totals = tuple((former + latter for former, latter in zip(totals, weight_rows)))
        return (totals, (result.astype(jnp.bfloat16), input_rows.astype(jnp.bfloat16)))
    initial = tuple((jnp.zeros(matrix.shape, jnp.float32) for matrix in weights))
    totals, (outputs, inputs_back) = lax.scan(advance, initial, (encoder_input.reshape(block_count, block_chips, VIS, DE), visible_patches.reshape(block_count, block_chips, VIS), sensor_index.reshape(block_count, block_chips), cotangent.reshape(block_count, block_chips, PATCH, DD)))
    return (outputs.reshape(CHIPS, PATCH, DD), inputs_back.reshape(CHIPS, VIS, DE), totals[0], totals[1], totals[2], totals[3], totals[4], totals[5], totals[6], totals[7], totals[8], totals[9], totals[10], totals[11], totals[12], totals[13])
```

```python
import functools
import math
from types import SimpleNamespace

import jax
import jax.numpy as jnp
import numpy as np
from jax import lax
from jax.experimental import pallas as pl
from jax.experimental.pallas import tpu as pltpu
from jax.sharding import PartitionSpec as P

HD = 64
SMALL = 8
SIDE = 2
STAGES, COMPUTE = 8, 1000
MESH = pl.DeviceIdType.MESH
BF16, F32 = jnp.bfloat16, jnp.float32

epsilon = 1e-05


def positions(patch_count, model_width):
    half_width = model_width // 2
    places = np.arange(patch_count, dtype=np.float32)[:, None]
    frequency = np.exp(
        np.arange(half_width, dtype=np.float32) * np.float32(-math.log(10000.0) / half_width)
    )
    angles = places * frequency[None, :]
    return np.concatenate([np.sin(angles), np.cos(angles)], axis=1)


VMEM = pl.BlockSpec(memory_space=pltpu.VMEM)
ANYWHERE = pl.BlockSpec(memory_space=pl.ANY)


def call_kernel(body, inputs, outs, scratch, name, limit, special):
    trees = [
        {key: value for key, (_, value) in inputs.items()},
        {key: value for key, (_, value) in outs.items()},
        scratch,
    ]
    flat = [jax.tree.flatten(tree) for tree in trees]
    sizes = [len(leaves) for leaves, _ in flat]

    def specs(group, tree):
        spread = {key: jax.tree.map(lambda _: group[key][0], tree[key]) for key in tree}
        return jax.tree.leaves(spread)

    def kernel(*refs):
        fields, begin = {}, 0
        for size, (_, definition) in zip(sizes, flat):
            fields.update(jax.tree.unflatten(definition, refs[begin : begin + size]))
            begin += size
        body(SimpleNamespace(**fields))

    results = pl.pallas_call(
        kernel,
        out_shape=flat[1][0],
        in_specs=specs(inputs, trees[0]),
        out_specs=specs(outs, trees[1]),
        scratch_shapes=flat[2][0],
        compiler_params=pltpu.CompilerParams(vmem_limit_bytes=limit * 2**20, **special),
        name=name,
    )(*flat[0][0])
    return SimpleNamespace(**jax.tree.unflatten(flat[1][1], results))


def shaped(shape, kind=BF16):
    return jax.ShapeDtypeStruct(shape, kind)


class Place:
    def __init__(self, depth):
        group, member = lax.axis_index("dp"), lax.axis_index("seq")
        self.depth = depth
        self.z, self.x = group // SIDE, lax.rem(group, SIDE)
        self.y, self.c = member // SIDE, lax.rem(member, SIDE)

    def device(self, z=None, x=None, y=None, c=None):
        z = self.z if z is None else z
        x = self.x if x is None else x
        y = self.y if y is None else y
        c = self.c if c is None else c
        return (z * SIDE + x, y * SIDE + c)

    def across(self, axis):
        if axis == "x":
            return self.device(x=1 - self.x)
        if axis == "y":
            return self.device(y=1 - self.y)
        return self.device(c=1 - self.c)

    def greet(self):
        barrier = pltpu.get_barrier_semaphore()

        def hail(device):
            pl.semaphore_signal(barrier, inc=1, device_id=device, device_id_type=MESH)

        for axis in "xyc":
            hail(self.across(axis))
        guarded(lambda: self.z > 0, lambda: hail(self.device(z=self.z - 1)))
        guarded(lambda: self.z < self.depth - 1, lambda: hail(self.device(z=self.z + 1)))
        inner = (self.z > 0) & (self.z < self.depth - 1)
        pl.semaphore_wait(barrier, jnp.where(inner, 5, 4))


def guarded(condition, action):
    if condition is None:
        action()
    else:
        pl.when(condition())(action)


class Links:
    def __init__(self, send_sems, recv_sems):
        self.send_sems, self.recv_sems, self.sent = send_sems, recv_sems, []

    def make(self, part, slot, source, target, device):
        return pltpu.make_async_remote_copy(
            src_ref=source,
            dst_ref=target,
            send_sem=self.send_sems.at[part, slot],
            recv_sem=self.recv_sems.at[part, slot],
            device_id=device,
            device_id_type=MESH,
        )

    def send(self, condition, part, slot, views, device):
        guarded(condition, lambda: self.make(part, slot, *views(), device()).start())
        self.sent.append(
            (condition, lambda: self.make(part, slot, *views(), device()).wait_send())
        )

    def receive(self, part, slot, view, device):
        self.make(part, slot, view, view, device).wait_recv()

    def settle(self):
        for condition, action in self.sent:
            guarded(condition, action)


def slot_of(depth, kind, step=1):
    first = dict(x=0, y=1, c=2, up=3, down=3 + depth - 1)[kind]
    return first + step - 1


def slot_count(depth):
    return 3 + 2 * (depth - 1)


class Plan:
    def __init__(self, order):
        self.spots = {event: float(spot) for spot, event in enumerate(order)}
        self.events = []

    def stage(self, part, number, action):
        self.add(self.spots[part * STAGES + number], action)

    def add(self, spot, action):
        self.events.append((spot, len(self.events), action))

    def run(self, until=math.inf):
        self.events.sort(key=lambda event: event[:2])
        while self.events and self.events[0][0] < until:
            self.events.pop(0)[2]()


def chained(*actions):
    def run():
        for action in actions:
            action()

    return run


def plan_gather(plan, depth, parts, at):
    shards, wholes, halves, others = at.shards, at.held, at.halves, at.others
    count = len(wholes)
    place = Place(depth)
    z, x, y, c = place.z, place.x, place.y, place.c
    links = Links(at.send_sems, at.recv_sems)
    place.greet()
    swaps = []
    for k in range(count):
        width = halves[k].shape[1]
        far = pl.ds(pl.multiple_of((1 - c) * width, 128), width)
        halves[k][...] = shards[k][:, far].astype(F32)
        swaps.append(
            pltpu.make_async_remote_copy(
                src_ref=halves[k],
                dst_ref=others[k],
                send_sem=at.first_send.at[k],
                recv_sem=at.first_recv.at[k],
                device_id=place.across("c"),
                device_id_type=MESH,
            )
        )
        swaps[k].start()

    def open_block(k):
        width = halves[k].shape[1]
        near = pl.ds(pl.multiple_of(c * width, 128), width)
        mine = shards[k][:, near].astype(F32)
        swaps[k].wait_recv()
        theirs = others[k][...]
        low_rows = jnp.where(c == 0, mine, theirs)
        high_rows = jnp.where(c == 0, theirs, mine)
        wholes[k][z, x, y, :, near] = jnp.concatenate([low_rows, high_rows], axis=0).astype(BF16)

    opened = set()

    def table(part, k, row, rows, order):
        width = halves[k].shape[1]

        def region(done, core=c, **spot):
            where = {**dict(z=z, x=x, y=y), **spot}
            sizes = dict(z=depth, x=SIDE, y=SIDE)
            lead = [pl.ds(0, sizes[a]) if a in done else where[a] for a in "zxy"]
            columns = pl.ds(pl.multiple_of(core * width, 128), width)
            return wholes[k].at[(*lead, pl.ds(row, rows), columns)]

        def send(condition, kind, step, view, device):
            links.send(
                condition, part, slot_of(depth, kind, step), lambda: (view(), view()), device
            )

        def begin():
            if k not in opened:
                opened.add(k)
                open_block(k)

        done, starters = "", []
        for axis in order + "c":
            here = done
            if axis == "z":

                def start(here=here):
                    send(lambda: z < depth - 1, "up", 1, lambda: region(here), lambda: place.device(z=z + 1))
                    send(lambda: z > 0, "down", 1, lambda: region(here), lambda: place.device(z=z - 1))

                def hop(step, here=here):
                    def below():
                        return region(here, z=z - step)

                    def above():
                        return region(here, z=z + step)

                    @pl.when(z >= step)
                    def _():
                        links.receive(
                            part, slot_of(depth, "up", step), below(), place.device(z=z - 1)
                        )

                    if step < depth - 1:
                        send(
                            lambda: (z >= step) & (z < depth - 1),
                            "up",
                            step + 1,
                            below,
                            lambda: place.device(z=z + 1),
                        )

                    @pl.when(z < depth - step)
                    def _():
                        links.receive(
                            part, slot_of(depth, "down", step), above(), place.device(z=z + 1)
                        )

                    if step < depth - 1:
                        send(
                            lambda: (z < depth - step) & (z > 0),
                            "down",
                            step + 1,
                            above,
                            lambda: place.device(z=z - 1),
                        )

                waits = [functools.partial(hop, step) for step in range(1, depth)]
            else:

                def start(axis=axis, here=here):
                    send(None, axis, 1, lambda: region(here), lambda: place.across(axis))

                def arrive(axis=axis, here=here):
                    if axis == "c":
                        view = region(here, core=1 - c)
                    else:
                        view = region(here, **{axis: 1 - (x if axis == "x" else y)})
                    links.receive(part, slot_of(depth, axis), view, place.across(axis))

                waits = [arrive]
            starters.append((start, waits))
            done += axis
        stages = [chained(begin, starters[0][0])]
        for number, (_, waits) in enumerate(starters):
            stages += waits
            if number + 1 < len(starters):
                stages[-1] = chained(stages[-1], starters[number + 1][0])
        return stages

    for number, part in enumerate(parts):
        for stage, action in enumerate(table(number, *part)):
            plan.stage(number, stage, action)

    def finish():
        for swap in swaps:
            swap.wait_send()
        links.settle()

    return finish


def add_rows(target, source):
    target[...] = target[...] + source[...]


def plan_scatter(plan, depth, parts, at, staging):
    fulls, works, others, sums = at.fulls, at.works, at.others, at.sums
    place = Place(depth)
    z, x, y, c = place.z, place.x, place.y, place.c
    links = Links(at.send_sems, at.recv_sems)
    place.greet()
    sizes = dict(z=depth, x=SIDE, y=SIDE)
    own = dict(z=z, x=x, y=y)
    kept = [sum(part[0] == k for part in parts) for k in range(len(sums))]

    def table(part, k, row, rows, order):
        width = works[k].shape[-1]
        window = pl.ds(row, rows)
        box = at.boxes[part]

        def box_of(kind, target):
            return box[kind].at[target - 1 if kind == "up" else target]

        def columns(core):
            return pl.ds(pl.multiple_of(core * width, 128), width)

        every = (pl.ds(0, depth), pl.ds(0, SIDE), pl.ds(0, SIDE))

        def copy_near():
            return pltpu.make_async_copy(
                fulls[k].at[(*every, window, columns(c))],
                works[k].at[(*every, window)],
                at.local_sem.at[part],
            )

        def begin():
            staging.settle(k)
            copy_near().start()
            links.send(
                None,
                part,
                slot_of(depth, "c"),
                lambda: (
                    fulls[k].at[(*every, window, columns(1 - c))],
                    others[k].at[(*every, window)],
                ),
                lambda: place.across("c"),
            )

        def region(left, **spot):
            where = {**own, **spot}
            lead = [pl.ds(0, sizes[a]) if a in left else where[a] for a in "zxy"]
            return works[k].at[(*lead, window)]

        def add_region(left, source, **spot):
            where = {**own, **spot}
            names = [a for a in "zxy" if a in left]

            def body(index, carry):
                places, rest = {}, index
                for a in reversed(names):
                    places[a] = lax.rem(rest, sizes[a])
                    rest = rest // sizes[a]
                lead = tuple(places.get(a, where[a]) for a in "zxy")
                piece = source.at[tuple(places[a] for a in names)] if names else source
                add_rows(works[k].at[(*lead, window)], piece)
                return carry

            lax.fori_loop(0, math.prod(sizes[a] for a in names), body, 0)

        def join():
            copy_near().wait()
            view = others[k].at[(*every, window)]
            links.receive(part, slot_of(depth, "c"), view, place.across("c"))
            add_region("zxy", view)

        def start_axis(axis, left):
            def run():
                links.send(
                    None,
                    part,
                    slot_of(depth, axis),
                    lambda: (region(left, **{axis: 1 - own[axis]}), box[axis]),
                    lambda: place.across(axis),
                )

            return run

        def finish_axis(axis, left):
            def run():
                links.receive(part, slot_of(depth, axis), box[axis], place.across(axis))
                add_region(left, box[axis])

            return run

        def line(hop, left):
            def send(kind, step, target, device):
                spot = hop if kind == "up" else depth - 1 - hop
                links.send(
                    lambda: z == spot,
                    part,
                    slot_of(depth, kind, step),
                    lambda: (region(left, z=target), box_of(kind, target)),
                    device,
                )

            def take(kind):
                spot = hop if kind == "up" else depth - 1 - hop
                targets = range(depth - 1, hop - 1, -1) if kind == "up" else range(spot + 1)
                back = place.device(z=z - 1 if kind == "up" else z + 1)

                @pl.when(z == spot)
                def _():
                    for target in targets:
                        step = target if kind == "up" else depth - 1 - target
                        links.receive(
                            part, slot_of(depth, kind, step), box_of(kind, target), back
                        )
                        if target != spot:
                            add_region(left, box_of(kind, target), z=target)

            def run():
                if hop > 0:
                    take("up")
                    take("down")
                for target in range(depth - 1, hop, -1):
                    send("up", target, target, lambda: place.device(z=z + 1))
                for target in range(0, depth - 1 - hop):
                    send("down", depth - 1 - target, target, lambda: place.device(z=z - 1))

            return run

        def finish_line(left):
            def run():
                @pl.when(z > 0)
                def _():
                    add_region(left, box_of("up", z))

                @pl.when(z < depth - 1)
                def _():
                    add_region(left, box_of("down", z))

            return run

        def keep():
            sums[k][window, :] = works[k][z, x, y, window].astype(F32)
            kept[k] -= 1
            if kept[k] == 0:
                swap_rows(place, at, k, True)

        left, stages, pending = "zxy", [begin], [join]
        for axis in order:
            left = left.replace(axis, "")
            if axis == "z":
                stages.append(chained(*pending, line(0, left)))
                stages += [line(hop, left) for hop in range(1, depth)]
                pending = [finish_line(left)]
            else:
                stages.append(chained(*pending, start_axis(axis, left)))
                pending = [finish_axis(axis, left)]
        return stages + [chained(*pending, keep)]

    for number, part in enumerate(parts):
        for stage, action in enumerate(table(number, *part)):
            plan.stage(number, stage, action)

    def finish():
        for k in range(len(sums)):
            swap_rows(place, at, k, False)
        links.settle()

    return finish


def swap_rows(place, at, k, begin):
    c, shard, total = place.c, at.shards[k], at.sums[k]
    rows, width = shard.shape[0], total.shape[1]
    near = pl.ds(pl.multiple_of(c * width, 128), width)
    far = pl.ds(pl.multiple_of((1 - c) * width, 128), width)
    mine = pl.ds(pl.multiple_of(c * rows, 8), rows)
    theirs = pl.ds(pl.multiple_of((1 - c) * rows, 8), rows)

    def swap(columns):
        return pltpu.make_async_remote_copy(
            src_ref=total.at[theirs],
            dst_ref=shard.at[:, columns],
            send_sem=at.last_send.at[k],
            recv_sem=at.last_recv.at[k],
            device_id=place.across("c"),
            device_id_type=MESH,
        )

    if begin:
        swap(near).start()
        shard[:, near] = total[mine, :]
    else:
        swap(far).wait_recv()
        swap(near).wait_send()


def scatter_scratch(depth, parts, halves):
    boxes = []
    for k, _, rows, order in parts:
        left, box = "zxy", {}
        for axis in order:
            left = left.replace(axis, "")
            shape = (*(depth if a == "z" else SIDE for a in left), rows, halves[k][1])
            if axis == "z":
                box.update(dict.fromkeys(("up", "down"), pltpu.VMEM((depth - 1, *shape), BF16)))
            else:
                box[axis] = pltpu.VMEM(shape, BF16)
        boxes.append(box)
    grid = (depth, SIDE, SIDE)
    many = pltpu.SemaphoreType.DMA((len(parts), slot_count(depth)))
    few = pltpu.SemaphoreType.DMA((len(halves),))
    return dict(
        works=[pltpu.VMEM((*grid, *half), BF16) for half in halves],
        others=[pltpu.VMEM((*grid, *half), BF16) for half in halves],
        sums=[pltpu.VMEM(half, F32) for half in halves],
        boxes=boxes,
        local_sem=pltpu.SemaphoreType.DMA((len(parts),)),
        last_send=few,
        last_recv=few,
        send_sems=many,
        recv_sems=many,
    )


def times(left, right):
    return jnp.dot(left, right, preferred_element_type=F32)


def times_back(left, right):
    return lax.dot_general(left, right, (((1,), (1,)), ((), ())), preferred_element_type=F32)


def back_times(left, right):
    return lax.dot_general(left, right, (((0,), (0,)), ((), ())), preferred_element_type=F32)


def low(value):
    return value.astype(BF16)


def wide(value):
    return value.astype(F32)


def flat(blocks):
    return blocks.reshape(-1, blocks.shape[-1])


def gelu_pair(v):
    root, cubic = math.sqrt(2.0 / math.pi), 0.044715
    square = v * v
    bent = jnp.tanh(v * (root + (root * cubic) * square))
    half = 0.5 + 0.5 * bent
    active = v * half
    slope = half + active * (1.0 - half) * (2.0 * root + (6.0 * root * cubic) * square)
    return active, slope


def unit_of(stream):
    centred = stream - jnp.mean(stream, axis=-1, keepdims=True)
    inverse = lax.rsqrt(jnp.mean(centred * centred, axis=-1, keepdims=True) + epsilon)
    return centred * inverse, inverse


def norm_gradient(gradient, normed, inverse, gain):
    scaled = gradient * gain
    first = jnp.mean(scaled, axis=-1, keepdims=True)
    second = jnp.mean(scaled * normed, axis=-1, keepdims=True)
    return inverse * (scaled - first - normed * second)


def column_sum(value):
    return jnp.sum(value, axis=0, keepdims=True)


def head_masks():
    lanes = lax.broadcasted_iota(jnp.int32, (1, 2 * HD), 1)
    first = jnp.where(lanes < HD, 1.0, 0.0)
    return (low(first), low(1.0 - first)), lanes < HD


def pair_lanes(pair, width):
    return [pl.ds(k * width + 2 * HD * pair, 2 * HD) for k in range(3)]


def softmax_pairs(triples, fence=None):
    masks, first = head_masks()
    masks = [mask * (1.0 / math.sqrt(HD)) for mask in masks]
    heads = [(triple, mask) for triple in triples for mask in masks]
    scores = [times_back(queries * mask, key_set) for (queries, key_set, _), mask in heads]
    if fence is not None:
        scores = [jnp.where(fence, score, -1e30) for score in scores]
    raised = [jnp.exp(score - jnp.max(score, axis=-1, keepdims=True)) for score in scores]
    softs = [low(up * (1.0 / jnp.sum(up, axis=-1, keepdims=True))) for up in raised]
    mixed = [times(soft, values) for soft, ((_, _, values), _) in zip(softs, heads)]
    return [
        (softs[k : k + 2], low(jnp.where(first, mixed[k], mixed[k + 1])))
        for k in range(0, len(heads), 2)
    ]


def softmax_pairs_back(items):
    masks, first = head_masks()
    heads = [(item, k) for item in items for k in range(2)]
    soft_grads = [times_back(item[0] * masks[k], item[4]) for item, k in heads]
    wides = [wide(item[1][k]) for item, k in heads]
    weighted = [soft * grad for soft, grad in zip(wides, soft_grads)]
    score_grads = [
        low(value - soft * jnp.sum(value, axis=-1, keepdims=True))
        for value, soft in zip(weighted, wides)
    ]
    query_grads = [times(grad, item[3]) for grad, (item, _) in zip(score_grads, heads)]
    key_grads = [back_times(grad, item[2]) for grad, (item, _) in zip(score_grads, heads)]
    value_grads = [back_times(item[1][k], item[0]) for item, k in heads]
    factors = (1.0 / math.sqrt(HD), 1.0 / math.sqrt(HD), 1.0)
    return [
        [
            low(jnp.where(first, grads[k], grads[k + 1]) * factor)
            for grads, factor in zip((query_grads, key_grads, value_grads), factors)
        ]
        for k in range(0, len(heads), 2)
    ]


def chip_fence(size, length):
    rows = lax.broadcasted_iota(jnp.int32, (size, size), 0)
    columns = lax.broadcasted_iota(jnp.int32, (size, size), 1)
    return rows // length == columns // length


def spot_of(visible, chip, length):
    chosen = visible[chip : chip + 1, :]
    places = lax.broadcasted_iota(jnp.int32, (length, chosen.shape[1]), 0)
    return jnp.where(places == chosen, 1.0, 0.0)


def absent_of(placing):
    return 1.0 - jnp.sum(placing, axis=1, keepdims=True)


def owner_mask(shape, kind, width):
    rows = lax.broadcasted_iota(jnp.int32, shape, 0)
    lanes = lax.broadcasted_iota(jnp.int32, shape, 1)
    begin = (rows - kind) * (width // SMALL)
    return (lax.rem(rows, SMALL) == kind) & (lanes >= begin) & (lanes < begin + width)


def spread_small(tiles, kinds, width):
    total = tiles.shape[0] // SMALL * width
    lanes = lax.broadcasted_iota(jnp.int32, (tiles.shape[1], total), 1)
    places = lax.broadcasted_iota(jnp.int32, (tiles.shape[1], total), 0)
    spread = times(tiles, low(jnp.where(lax.rem(lanes, width) == places, 1.0, 0.0)))
    return [
        column_sum(jnp.where(owner_mask(spread.shape, kind, width), spread, 0.0))
        for kind in kinds
    ]


def collect_small(vectors, width, tile_lanes):
    lanes_all = next(iter(vectors.values())).shape[1]
    total = jnp.zeros((SMALL * (lanes_all // width), lanes_all), F32)
    for kind, vector in vectors.items():
        total = total + jnp.where(owner_mask(total.shape, kind, width), vector, 0.0)
    lanes = lax.broadcasted_iota(jnp.int32, (lanes_all, tile_lanes), 0)
    places = lax.broadcasted_iota(jnp.int32, (lanes_all, tile_lanes), 1)
    return times(low(total), low(jnp.where(lax.rem(lanes, width) == places, 1.0, 0.0)))


class Deck:
    def __init__(self, chunks):
        self.chunks = chunks
        self.attend, self.merge = (0, 1, 2), 3
        self.expand = tuple(range(4, 4 + chunks))
        self.reduce = 4 + chunks
        (
            self.narrow,
            self.later_attend,
            self.later_merge,
            self.later_expand,
            self.later_reduce,
            self.small,
        ) = range(self.reduce + 1, self.reduce + 7)
        self.count = self.small + 1
        self.squares = (*self.attend, self.merge, *self.expand)
        self.early = (*self.squares, self.reduce)

    def cut(self, groups, merge, expand, *rest):
        size = expand.shape[-1] // self.chunks
        views = [expand.at[..., pl.ds(k * size, size)] for k in range(self.chunks)]
        return [*groups, merge, *views, *rest]


def group_lanes(group, width):
    return [pl.ds(k * width + group * (width // 3), width // 3) for k in range(3)]


class Last:
    def __init__(self, count, action):
        self.count, self.action = count, action

    def __call__(self):
        self.count -= 1
        if self.count == 0:
            self.action()


class Keeper:
    def __init__(self, at):
        self.at, self.copies = at, []

    def __call__(self, *pairs):
        for source, target in pairs:
            sem = self.at.keep_sem.at[len(self.copies)]
            self.copies.append(pltpu.make_async_copy(source, target, sem))
            self.copies[-1].start()

    def settle(self):
        for copy in self.copies:
            copy.wait()


def front_pieces(at, deck, length, keep):
    rows, width = at.x.shape
    kept = at.kept
    held, chunks = at.held, deck.chunks
    block = 2 * length
    size = held[deck.expand[0]].shape[-1]

    def open_rows():
        unit, _ = unit_of(wide(at.x[...]))
        at.inner[...] = low(unit * at.early_gains[0:1, :])
        keep((at.inner, kept.inner))

    def project(number):
        matrix = flat(held[deck.attend[number]][...])
        packed = low(times(at.inner[...], matrix))
        for k, lanes in enumerate(group_lanes(number, width)):
            at.packed[:, lanes] = packed[:, k * (width // 3) : (k + 1) * (width // 3)]
        projected()

    def attend_group(number):
        fence = chip_fence(block, length)
        places = [
            (pair, pl.ds(group * block, block))
            for pair in range(number * pairs // 3, (number + 1) * pairs // 3)
            for group in range(rows // block)
        ]
        triples = [
            [at.packed[part, lanes] for lanes in pair_lanes(pair, width)] for pair, part in places
        ]
        for (pair, part), (softs, mixture) in zip(places, softmax_pairs(triples, fence)):
            for k in range(2):
                at.softs[2 * pair + k, part, :] = softs[k]
            at.mixed[part, pair_lanes(pair, width)[0]] = mixture
        attended()

    def enter_middle():
        middle = wide(at.x[...]) + times(at.mixed[...], flat(held[deck.merge][...]))
        at.middle[...] = middle
        at.total[...] = middle
        keep((at.middle, kept.middle))
        unit, _ = unit_of(middle)
        at.mid_inner[...] = low(unit * at.early_gains[1:2, :])
        keep((at.mid_inner, kept.mid_inner))

    def expand_reduce(number):
        columns = pl.ds(number * size, size)
        reduce_rows = held[deck.reduce].shape[0] // chunks
        reduce = flat(held[deck.reduce][pl.ds(number * reduce_rows, reduce_rows)])
        active, slope = gelu_pair(times(at.mid_inner[...], flat(held[deck.expand[number]][...])))
        active = low(active)
        at.hidden[:, columns] = active
        at.slope[:, columns] = low(slope)
        at.total[...] += times(active, reduce)
        expanded()

    def leave():
        at.encoded[...] = low(at.total[...])
        keep((at.encoded, kept.encoded))

    pairs = width // (2 * HD)
    projected = Last(3, lambda: keep((at.packed, kept.packed)))
    attended = Last(3, lambda: keep((at.softs, kept.softs), (at.mixed, kept.mixed)))
    expanded = Last(chunks, lambda: keep((at.hidden, kept.hidden), (at.slope, kept.slope)))
    pieces = [((deck.small,), open_rows)]
    for k in range(3):
        pieces.append(((deck.attend[k],), functools.partial(project, k)))
        pieces.append(((), functools.partial(attend_group, k)))
    pieces += [((deck.merge,), enter_middle)]
    pieces += [
        ((deck.expand[k], deck.reduce), functools.partial(expand_reduce, k)) for k in range(chunks)
    ]
    return pieces + [((), leave)]


def later_front_pieces(at, deck, keep):
    chips, length, model = at.cotangent.shape
    held, small = at.held, at.later_small
    visible_count = at.visible.shape[1]
    width = at.later_mixed.shape[1]
    chunk = held[deck.later_reduce].shape[3] * SIDE
    kept = at.kept
    merge_rows = held[deck.later_merge]

    def rows_of(chip):
        return pl.ds(chip * length, length)

    def narrow():
        for copy in at.late:
            copy.wait()
        at.narrowed[...] = low(times(at.encoded[...], flat(held[deck.narrow][...])))

    def open_chip(chip):
        placing = spot_of(at.visible, chip, length)
        filler = jnp.zeros((1, model), F32)
        for number in range(SMALL - 4):
            chosen = jnp.where(at.sensors[chip] == number, 1.0, 0.0)
            filler = filler + chosen * small[4 + number : 5 + number, :]
        seen = at.narrowed[pl.ds(chip * visible_count, visible_count), :]
        placed = low(times(low(placing), seen) + absent_of(placing) * filler + at.spots[...])
        at.stream[rows_of(chip), :] = placed
        unit, _ = unit_of(wide(placed))
        inner = low(unit * small[0:1, :])
        at.open_inner[rows_of(chip), :] = inner
        at.later_packed[rows_of(chip), :] = low(times(inner, flat(held[deck.later_attend][...])))
        opened()

    def attend_chip(chip):
        rows = rows_of(chip)
        lanes = [pair_lanes(pair, width) for pair in range(width // (2 * HD))]
        triples = [[at.later_packed[rows, lane] for lane in three] for three in lanes]
        for pair, triple in enumerate(triples):
            ((softs, mixture),) = softmax_pairs([triple])
            for k in range(2):
                at.later_softs[chip, 2 * pair + k] = softs[k]
            at.later_mixed[rows, lanes[pair][0]] = mixture
        attended()

    def middle_chip(chip):
        rows = rows_of(chip)
        merge = flat(merge_rows[...])
        middle = wide(at.stream[rows, :]) + times(at.later_mixed[rows, :], merge)
        at.later_middle_grad[rows, :] = middle
        unit, _ = unit_of(middle)
        inner = low(unit * small[1:2, :])
        at.later_inner[rows, :] = inner
        at.later_turned[:, rows] = inner.T

    def hidden_chunk(number, carry):
        begin = pl.multiple_of(number * chunk, chunk)
        part = pl.ds(begin, chunk)
        matrix = flat(held[deck.later_expand][..., part])
        reduce = held[deck.later_reduce]
        lines = reduce.shape[3]
        group = number * chunk // lines
        spot = (group // (SIDE * SIDE), lax.rem(group // SIDE, SIDE))
        back = flat(reduce[(*spot, slice(None), slice(None), slice(None))])
        upstream = flat(at.cotangent[...])
        active, slope = gelu_pair(times(at.later_inner[...], matrix))
        active = low(active)
        at.later_hidden[:, part] = active
        at.reduce_grad[part, :] = low(back_times(active, upstream))
        change = low(times_back(upstream, back) * slope)
        at.later_hidden_grad[:, part] = change
        at.expand_grad[:, part] = low(times(at.later_turned[...], change))
        return carry

    def run_hidden():
        lax.fori_loop(0, at.reduce_grad.shape[0] // chunk, hidden_chunk, 0)
        keep((at.reduce_grad, kept.reduce_grad), (at.expand_grad, kept.expand_grad))

    def leave():
        at.small_grad[...] = jnp.zeros_like(at.small_grad)

        def chip_rows(chip, carry):
            rows = pl.ds(pl.multiple_of(chip * length, length), length)
            middle = at.later_middle_grad[rows, :]
            reduce = flat(held[deck.later_reduce][...])
            at.decoded[chip] = low(middle + times(at.later_hidden[rows, :], reduce))
            unit, inverse = unit_of(middle)
            expand = flat(held[deck.later_expand][...])
            change = times_back(at.later_hidden_grad[rows, :], expand)
            at.small_grad[1:2, :] += column_sum(change * unit)
            at.later_middle_grad[rows, :] = wide(at.cotangent[chip]) + norm_gradient(
                change, unit, inverse, small[1:2, :]
            )
            return carry

        lax.fori_loop(0, chips, chip_rows, 0)

    opened = Last(
        chips,
        lambda: keep(
            (at.stream, kept.stream),
            (at.later_packed, kept.later_packed),
            (at.open_inner, kept.open_inner),
        ),
    )
    attended = Last(
        chips,
        lambda: keep((at.later_softs, kept.later_softs), (at.later_mixed, kept.later_mixed)),
    )
    pieces = [((deck.narrow,), narrow)]
    for chip in range(chips):
        pieces.append(((deck.later_attend,), functools.partial(open_chip, chip)))
        pieces.append(((), functools.partial(attend_chip, chip)))
        pieces.append(((deck.later_merge,), functools.partial(middle_chip, chip)))
    needs = (deck.later_expand, deck.later_reduce)
    return pieces + [(needs, run_hidden), ((), leave)]


def unpack_small(at, deck, owned):
    tiles = flat(at.held[deck.small][...])[:, :128]
    early = spread_small(tiles, (0, 1), owned[0])
    later = spread_small(tiles, range(2, SMALL), owned[1])
    at.early_gains[...] = jnp.zeros_like(at.early_gains)
    at.later_small[...] = jnp.zeros_like(at.later_small)
    for row, value in zip((0, 1), early):
        at.early_gains[row : row + 1, :] = value
    for row, value in zip((0, 1, 4, 5, 6, 7), later):
        at.later_small[row : row + 1, :] = value


def pack_small(at):
    at.tile[...] = jnp.zeros_like(at.tile)
    for row, vector in enumerate(at.smalls[:4]):
        lanes = vector.shape[0]
        at.tile[row : row + 1, 0:lanes] = wide(vector[...]).reshape(1, lanes)
    tokens = at.smalls[4]
    at.tile[4:SMALL, 0 : tokens.shape[1]] = wide(tokens[...])


def front_body(depth, parts, order, deck, length, owned, at):
    plan, finish, ready, pieces = Plan(order), None, {}, []
    if parts is not None:
        pack_small(at)
        for k, group in enumerate(at.groups):
            third = group.shape[1] // 3
            for number, lanes in enumerate(group_lanes(k, group.shape[1])):
                group[:, number * third : (number + 1) * third] = at.shards[0][:, lanes]
        at.shards = deck.cut(at.groups, *at.shards[1:], at.tile)
        finish = plan_gather(plan, depth, parts, at)
        for number, part in enumerate(parts):
            last = plan.spots[number * STAGES + depth + 2]
            ready[part[0]] = max(ready.get(part[0], 0.0), last)
        pieces.append(((deck.small,), functools.partial(unpack_small, at, deck, owned)))
    at.kept = SimpleNamespace(**at.kept)
    at.late = [
        pltpu.make_async_copy(at.far_cotangent, at.cotangent, at.late_sem.at[0]),
        pltpu.make_async_copy(at.far_spots, at.spots, at.late_sem.at[1]),
    ]
    for copy in at.late:
        copy.start()
    keep = Keeper(at)
    pieces += front_pieces(at, deck, length, keep) + later_front_pieces(at, deck, keep)

    def move(k):
        ends = (at.wholes[k], at.held[k])
        if parts is not None:
            ends = ends[::-1]
        return pltpu.make_async_copy(*ends, at.load_sem.at[k])

    for k in range(len(at.wholes)):
        plan.add(ready.get(k, -1.0) + 0.5, move(k).start)
    waited = set()
    for number, (needs, action) in enumerate(pieces):
        time = plan.spots.get(COMPUTE + number, float(number))

        def piece(needs=needs, action=action):
            if parts is None:
                for k in set(needs) - waited - {deck.small}:
                    waited.add(k)
                    move(k).wait()
            action()

        assert all(ready.get(k, -1.0) < time for k in needs)
        plan.add(time, piece)
    plan.run()
    keep.settle()
    for k in set(range(len(at.wholes))) - waited:
        move(k).wait()
    if finish is not None:
        finish()


def run_front(x, data, weights, depth, parts, order, deck, owned):
    visible, sensors, cotangent = data[:3]
    chips, length, model = cotangent.shape
    rows, width = x.shape
    every = chips * length
    gathers = parts is not None
    scale = 2 if gathers else 1 / (depth * SIDE * SIDE)
    sizes = [(w.shape[0] * scale, w.shape[1]) for w in weights[:9]]
    sizes = [(depth, SIDE, SIDE, int(r), c) for r, c in sizes]
    attend, merge, expand, reduce, narrow, later_attend, later_merge, *later = sizes
    square, inside = merge, math.prod(later_merge[:4])
    blocks = [square] * (4 + deck.chunks) + [reduce, narrow, later_attend, later_merge, *later]
    hidden_width, later_hidden_width = expand[-1], later[0][-1]
    vmem, anywhere = VMEM, ANYWHERE
    inputs = dict(
        x=(vmem, x),
        visible=(vmem, visible),
        sensors=(pl.BlockSpec(memory_space=pltpu.SMEM), sensors),
        far_cotangent=(anywhere, cotangent),
        far_spots=(anywhere, positions(length, model)),
    )
    kept = dict(
        packed=shaped((rows, 3 * width)),
        softs=shaped((width // HD, rows, 2 * (rows // chips))),
        mixed=shaped((rows, width)),
        middle=shaped((rows, width), F32),
        hidden=shaped((rows, hidden_width)),
        slope=shaped((rows, hidden_width)),
        encoded=shaped((rows, width)),
        stream=shaped((every, model)),
        later_packed=shaped((every, 3 * inside)),
        later_softs=shaped((chips, inside // HD, length, length)),
        later_mixed=shaped((every, inside)),
        expand_grad=shaped((model, later_hidden_width)),
        reduce_grad=shaped((later_hidden_width, model)),
        inner=shaped((rows, width)),
        mid_inner=shaped((rows, width)),
        open_inner=shaped((every, model)),
    )
    outs = dict(
        later_middle_grad=shaped((every, model), F32),
        decoded=shaped(cotangent.shape),
        small_grad=shaped((SMALL, model), F32),
    )
    scratch = dict(
        total=((rows, width), F32),
        narrowed=((rows, model), BF16),
        later_inner=((every, model), BF16),
        later_turned=((model, every), BF16),
        later_hidden=((every, later_hidden_width), BF16),
        later_hidden_grad=((every, later_hidden_width), BF16),
    )
    scratch = {key: pltpu.VMEM(*value) for key, value in scratch.items()}
    scratch.update({key: pltpu.VMEM(value.shape, value.dtype) for key, value in kept.items()})
    scratch.update(
        keep_sem=pltpu.SemaphoreType.DMA((len(kept),)),
        cotangent=pltpu.VMEM(cotangent.shape, BF16),
        spots=pltpu.VMEM((length, model), F32),
        late_sem=pltpu.SemaphoreType.DMA((2,)),
    )
    special = {}
    if gathers:
        tile = (SMALL, 256)
        blocks.append((depth, SIDE, SIDE, 2 * SMALL, tile[1]))
        inputs.update(
            shards=(vmem, list(weights[:9])), smalls=(vmem, list(weights[9]))
        )
        outs.update(early_gains=shaped((SMALL, width), F32), later_small=shaped((SMALL, model), F32))
        halves = [
            pltpu.VMEM((block[3] // 2, block[4] // 2), F32) for block in blocks
        ]
        few = pltpu.SemaphoreType.DMA((deck.count,))
        many = pltpu.SemaphoreType.DMA((len(parts), slot_count(depth)))
        scratch.update(
            tile=pltpu.VMEM(tile, F32),
            groups=[pltpu.VMEM(weights[1].shape, BF16)] * 3,
            halves=halves,
            others=halves,
            first_send=few,
            first_recv=few,
            send_sems=many,
            recv_sems=many,
        )
        special = dict(collective_id=0, has_side_effects=True)
    else:
        inputs.update(early_gains=(vmem, data[3]), later_small=(vmem, data[4]))
    outs = {key: (vmem, value) for key, value in outs.items()}
    outs.update(kept=(anywhere, kept))
    if gathers:
        kept = blocks[: deck.later_merge + 1]
        outs.update(wholes=(anywhere, [shaped(block) for block in kept]))
    else:
        inputs.update(wholes=(anywhere, [w.reshape(b) for w, b in zip(square_up(weights, deck), blocks)]))
    scratch.update(
        held=[pltpu.VMEM(block, BF16) for block in blocks],
        load_sem=pltpu.SemaphoreType.DMA((deck.count,)),
    )
    body = functools.partial(front_body, depth, parts, order, deck, rows // chips, owned)
    results = call_kernel(body, inputs, outs, scratch, "front", 62, special)
    vars(results).update(results.kept)
    return results


def square_up(weights, deck):
    attend, merge, expand, *rest = weights
    width = merge.shape[1]
    thirds = attend.reshape(-1, 3, 3, width // 3)
    groups = [thirds[:, :, k].reshape(-1, width) for k in range(3)]
    return [*groups, merge, *jnp.split(expand, deck.chunks, axis=1), *rest]


class Staging:
    def __init__(self, at):
        self.at, self.used, self.open = at, {}, {}

    def put(self, kind, value, k, where=...):
        slots = self.at.outlets[kind]
        slot = self.used.get(kind, 0) % slots.shape[0]
        self.used[kind] = self.used.get(kind, 0) + 1
        for entries in self.open.values():
            for entry in [e for e in entries if e[0] == (kind, slot)]:
                entry[1]().wait()
                entries.remove(entry)
        slots[slot] = low(value).reshape(slots.shape[1:])

        def copy():
            return pltpu.make_async_copy(
                slots.at[slot], self.at.fulls[k].at[where], self.at.outlet_sems[kind].at[slot]
            )

        copy().start()
        self.open.setdefault(k, []).append(((kind, slot), copy))

    def settle(self, k):
        for _, copy in self.open.pop(k, []):
            copy().wait()


class Arrivals:
    def __init__(self, at):
        self.at, self.left = at, {}

    def start(self, sources, targets, sems):
        for number, key in enumerate(sources):
            self.left[key] = pltpu.make_async_copy(sources[key], targets[key], sems.at[number])
            self.left[key].start()

    def use(self, *keys):
        for key in keys:
            if key in self.left:
                self.left.pop(key).wait()


def later_back_pieces(at, deck, staging, arrivals):
    chips, length = at.chips, at.length
    small = at.later_small
    visible_count = at.visible.shape[1]
    name = SimpleNamespace

    def rows_of(chip):
        return pl.ds(chip * length, length)

    def attend_chip(chip):
        here = at.here
        width = here.mixed.shape[1]
        rows = rows_of(chip)
        arrivals.use((1, chip), 2, (3, chip), (4, chip))
        branch = low(here.middle_grad[rows, :])
        here.branch[rows, :] = branch
        mixture_grad = low(times_back(branch, here.merge[...]))
        lanes = [pair_lanes(pair, width) for pair in range(width // (2 * HD))]
        items = [
            (
                mixture_grad[:, 2 * HD * pair : 2 * HD * (pair + 1)],
                [here.softs[chip, 2 * pair + k] for k in range(2)],
                *(here.packed[rows, lane] for lane in three),
            )
            for pair, three in enumerate(lanes)
        ]
        for three, grads in zip(lanes, softmax_pairs_back(items)):
            for lane, grad in zip(three, grads):
                here.packed_grad[rows, lane] = grad

    def give_merge():
        arrivals.use(5)
        here = at.here
        staging.put("merge", back_times(here.mixed[...], here.branch[...]), deck.later_merge)

    def give_attend():
        here = at.here
        arrivals.use(0)
        staging.put("attend", back_times(here.inner[...], here.packed_grad[...]), deck.later_attend)

    def close_chip(chip):
        here = at.here
        rows = rows_of(chip)
        arrivals.use(6, 9)
        change = times_back(here.packed_grad[rows, :], here.attend[...])
        unit, inverse = unit_of(wide(here.stream[rows, :]))
        at.small_total[0:1, :] += column_sum(change * unit)
        placed_grad = low(
            here.middle_grad[rows, :] + norm_gradient(change, unit, inverse, small[0:1, :])
        )
        placing = spot_of(at.visible, chip, length)
        seen = pl.ds(chip * visible_count, visible_count)
        here.narrowed_grad[seen, :] = low(back_times(low(placing), placed_grad))
        masked = column_sum(absent_of(placing) * wide(placed_grad))
        for number in range(SMALL - 4):
            chosen = jnp.where(at.sensors[chip] == number, 1.0, 0.0)
            at.small_total[4 + number : 5 + number, :] += chosen * masked

    def give_narrow():
        here = at.here
        arrivals.use(7, 8)
        narrowed_grad = here.narrowed_grad[...]
        staging.put("narrow", back_times(here.encoded[...], narrowed_grad), deck.narrow)
        at.encoded_grad[...] = times_back(narrowed_grad, here.narrow[...])

    pieces = [(functools.partial(attend_chip, chip), ()) for chip in range(chips)]
    pieces += [(give_merge, (deck.later_merge,))]
    pieces += [(give_attend, (deck.later_attend,))]
    pieces += [(functools.partial(close_chip, chip), ()) for chip in range(chips)]
    return pieces + [(give_narrow, (deck.narrow,))]


def back_pieces(at, deck, staging, arrivals, owned):
    rows, width = at.encoded_grad.shape
    chunks, block = deck.chunks, at.block
    size = at.hidden_width // chunks
    squares = [*deck.expand, deck.merge, *deck.attend]

    def square(index, begin=False):
        here = at.here
        slot = index % here.squares.shape[0]
        copy = pltpu.make_async_copy(
            at.matrices[squares[index]], here.squares.at[slot], here.square_sems.at[slot]
        )
        copy.start() if begin else copy.wait()
        return here.squares.at[slot]

    def tall(index, begin=False):
        here = at.here
        slot = index % here.talls.shape[0]
        copy = pltpu.make_async_copy(
            at.matrices[deck.reduce].at[pl.ds(index * size, size)],
            here.talls.at[slot],
            here.tall_sems.at[slot],
        )
        copy.start() if begin else copy.wait()
        return here.talls.at[slot]

    def free(action, index, last):
        if index < last:
            action(index, True)

    def open_rows():
        here = at.here
        for index in range(here.squares.shape[0]):
            square(index, True)
            tall(index, True)
        here.branch[...] = low(at.encoded_grad[...])
        here.change[...] = jnp.zeros_like(here.change)
        at.early_grads[...] = jnp.zeros_like(at.early_grads)

    def reduce_expand(number):
        here = at.here
        arrivals.use((12, number), (13, number), 17)
        columns = pl.ds(number * size, size)
        reduce, expand = tall(number), square(number)
        branch = here.branch[...]
        hidden_grad = low(times_back(branch, reduce[...]) * wide(here.slope[:, columns]))
        here.change[...] += times_back(hidden_grad, expand[...])
        if number == 0:
            here.turned[...] = here.mid_inner[...].T
        staging.put("square", times(here.turned[...], hidden_grad), deck.expand[number])
        reduce_rows = at.fulls[deck.reduce].shape[0] // chunks
        staging.put(
            "tall",
            back_times(here.hidden[:, columns], branch),
            deck.reduce,
            pl.ds(number * reduce_rows, reduce_rows),
        )
        free(tall, number + here.talls.shape[0], chunks)
        free(square, number + here.squares.shape[0], len(squares))

    def leave_middle():
        here = at.here
        arrivals.use(11)
        unit, inverse = unit_of(here.middle[...])
        change = here.change[...]
        at.early_grads[1:2, :] = column_sum(change * unit)
        total = at.encoded_grad[...] + norm_gradient(
            change, unit, inverse, at.early_gains[1:2, :]
        )
        here.middle_grad[...] = total
        branch = low(total)
        merge = square(chunks)
        here.branch[...] = low(times_back(branch, merge[...]))
        arrivals.use(14)
        staging.put("square", back_times(here.mixed[...], branch), deck.merge)
        free(square, chunks + here.squares.shape[0], len(squares))
        here.change[...] = jnp.zeros_like(change)

    def attend_group(number):
        here = at.here
        arrivals.use(15, 16)
        places = [
            (pair, pl.ds(group * block, block))
            for pair in range(number * pairs // 3, (number + 1) * pairs // 3)
            for group in range(rows // block)
        ]
        items = [
            (
                here.branch[part, pair_lanes(pair, width)[0]],
                [here.softs[2 * pair + k, part, :] for k in range(2)],
                *(here.packed[part, lanes] for lanes in pair_lanes(pair, width)),
            )
            for pair, part in places
        ]
        for (pair, part), grads in zip(places, softmax_pairs_back(items)):
            for lanes, grad in zip(pair_lanes(pair, width), grads):
                here.packed_grad[part, lanes] = grad

    def project(number):
        here = at.here
        index = chunks + 1 + number
        arrivals.use(18)
        attend = square(index)
        thirds = [here.packed_grad[:, lanes] for lanes in group_lanes(number, width)]
        packed_grad = jnp.concatenate(thirds, axis=1)
        if number == 0:
            here.turned[...] = here.inner[...].T
        staging.put("square", times(here.turned[...], packed_grad), deck.attend[number])
        here.change[...] += times_back(packed_grad, attend[...])
        free(square, index + here.squares.shape[0], len(squares))

    def close_rows():
        here = at.here
        arrivals.use(10)
        unit, inverse = unit_of(wide(here.x[...]))
        change = here.change[...]
        at.early_grads[0:1, :] = column_sum(change * unit)
        at.input_grad[...] = low(
            here.middle_grad[...]
            + norm_gradient(change, unit, inverse, at.early_gains[0:1, :])
        )
        if owned is not None:
            lanes = at.outlets["small"].shape[-1]
            early = {k: at.early_grads[k : k + 1, :] for k in range(2)}
            places = ((2, 0), (3, 1), (4, 4), (5, 5), (6, 6), (7, 7))
            later = {k: at.small_total[row : row + 1, :] for k, row in places}
            tiles = collect_small(early, owned[0], lanes)
            staging.put("small", tiles + collect_small(later, owned[1], lanes), deck.small)

    pieces = [(open_rows, ())]
    for k in range(chunks):
        done = (deck.expand[k], deck.reduce) if k == chunks - 1 else (deck.expand[k],)
        pieces.append((functools.partial(reduce_expand, k), done))
    pieces += [(leave_middle, (deck.merge,))]
    pairs = width // (2 * HD)
    for k in range(3):
        pieces.append((functools.partial(attend_group, k), ()))
        pieces.append((functools.partial(project, k), (deck.attend[k],)))
    return pieces + [(close_rows, (deck.small,))]


def back_body(depth, parts, order, deck, owned, sizes, at):
    vars(at).update(sizes)
    staging, arrivals = Staging(at), Arrivals(at)
    plan, finish, first_spot = Plan(order), None, {}
    if parts is not None:
        finish = plan_scatter(plan, depth, parts, at, staging)
        for number, part in enumerate(parts):
            first = plan.spots[number * STAGES]
            first_spot[part[0]] = min(first_spot.get(part[0], first), first)
    later = later_back_pieces(at, deck, staging, arrivals)
    pieces = later + back_pieces(at, deck, staging, arrivals, owned)
    for number, (action, done) in enumerate(pieces):
        time = plan.spots.get(COMPUTE + number, float(number))
        assert all(time < first_spot.get(k, time + 1.0) for k in done)
        plan.add(time, action)
    switch = plan.spots.get(COMPUTE + len(later), float(len(later)))
    at.small_total[...] = at.small_grad[...]
    chips, length, rows, width = at.chips, at.length, *at.encoded_grad.shape
    every, model = at.later_stream.shape

    def decoder(**local):
        at.here = SimpleNamespace(**local)
        here = at.here
        pairs = [
            (at.open_inner, here.inner),
            (at.later_middle_grad, here.middle_grad),
            (at.later_merge, here.merge),
            (at.later_softs, here.softs),
            (at.later_packed, here.packed),
            (at.later_mixed, here.mixed),
            (at.later_attend, here.attend),
            (at.encoded, here.encoded),
            (at.narrow, here.narrow),
            (at.later_stream, here.stream),
        ]
        sources, targets = {}, {}

        def bring(key, spot, where):
            sources[key], targets[key] = (ref.at[where] for ref in pairs[spot])

        bring(2, 2, ...)
        for chip in range(chips):
            rows_here = pl.ds(chip * length, length)
            bring((1, chip), 1, rows_here)
            bring((3, chip), 3, chip)
            bring((4, chip), 4, rows_here)
        for spot in (5, 0, 6, 9, 7, 8):
            bring(spot, spot, ...)
        arrivals.start(sources, targets, here.sems)
        plan.run(switch)

    size = at.hidden_width // deck.chunks

    def same(ref):
        return pltpu.VMEM(ref.shape, ref.dtype)

    pl.run_scoped(
        decoder,
        stream=same(at.later_stream),
        middle_grad=same(at.later_middle_grad),
        merge=same(at.later_merge),
        softs=same(at.later_softs),
        packed=same(at.later_packed),
        mixed=same(at.later_mixed),
        attend=same(at.later_attend),
        encoded=same(at.encoded),
        narrow=same(at.narrow),
        inner=same(at.open_inner),
        branch=pltpu.VMEM((every, model), BF16),
        packed_grad=same(at.later_packed),
        narrowed_grad=pltpu.VMEM((rows, model), BF16),
        sems=pltpu.SemaphoreType.DMA((7 + 3 * chips,)),
    )

    def encoder(**local):
        at.here = SimpleNamespace(**local)
        here = at.here
        pairs = [
            (at.x, here.x),
            (at.middle, here.middle),
            (at.slope, here.slope),
            (at.hidden, here.hidden),
            (at.mixed, here.mixed),
            (at.softs, here.softs),
            (at.packed, here.packed),
            (at.mid_inner, here.mid_inner),
            (at.inner, here.inner),
        ]
        sources, targets = {}, {}

        def bring(key, spot, where):
            sources[key], targets[key] = (ref.at[where] for ref in pairs[spot])

        for number in range(deck.chunks):
            columns = (slice(None), pl.ds(number * size, size))
            bring((12, number), 2, columns)
            bring((13, number), 3, columns)
            if number == 0:
                bring(17, 7, ...)
        for spot in (1, 4, 5, 6, 8, 0):
            bring(10 + spot, spot, ...)
        arrivals.start(sources, targets, here.sems)
        plan.run()
        for k in (*deck.early, deck.small):
            staging.settle(k)

    pl.run_scoped(
        encoder,
        x=same(at.x),
        middle=same(at.middle),
        slope=same(at.slope),
        hidden=same(at.hidden),
        mixed=same(at.mixed),
        softs=same(at.softs),
        packed=same(at.packed),
        inner=same(at.inner),
        mid_inner=same(at.mid_inner),
        turned=pltpu.VMEM((width, rows), BF16),
        branch=pltpu.VMEM((rows, width), BF16),
        change=pltpu.VMEM((rows, width), F32),
        middle_grad=pltpu.VMEM((rows, width), F32),
        packed_grad=same(at.packed),
        squares=pltpu.VMEM((2, width, width), BF16),
        talls=pltpu.VMEM((2, size, width), BF16),
        square_sems=pltpu.SemaphoreType.DMA((2,)),
        tall_sems=pltpu.SemaphoreType.DMA((2,)),
        sems=pltpu.SemaphoreType.DMA((7 + 2 * deck.chunks,)),
    )
    for k in (deck.narrow, deck.later_attend, deck.later_merge):
        staging.settle(k)
    if finish is not None:
        finish()


def run_back(front, x, data, matrices, depth, parts, order, deck, owned):
    visible, sensors, _, gains, later_small = data
    rows, width = x.shape
    chips, length = front.later_softs.shape[0], front.later_softs.shape[2]
    model = front.stream.shape[1]
    scatters = parts is not None
    vmem, anywhere = VMEM, ANYWHERE
    grid = (depth, SIDE, SIDE)

    def blocks(matrix):
        lines, columns = matrix.shape
        return (*grid, lines // (depth * SIDE * SIDE), columns)

    inputs = dict(
        visible=(vmem, visible),
        sensors=(pl.BlockSpec(memory_space=pltpu.SMEM), sensors),
        early_gains=(vmem, gains),
        later_small=(vmem, later_small),
        small_grad=(vmem, front.small_grad),
        x=(anywhere, x),
        packed=(anywhere, front.packed),
        softs=(anywhere, front.softs),
        mixed=(anywhere, front.mixed),
        middle=(anywhere, front.middle),
        hidden=(anywhere, front.hidden),
        slope=(anywhere, front.slope),
        inner=(anywhere, front.inner),
        mid_inner=(anywhere, front.mid_inner),
        open_inner=(anywhere, front.open_inner),
        encoded=(anywhere, front.encoded),
        later_stream=(anywhere, front.stream),
        later_packed=(anywhere, front.later_packed),
        later_softs=(anywhere, front.later_softs),
        later_mixed=(anywhere, front.later_mixed),
        later_middle_grad=(anywhere, front.later_middle_grad),
        matrices=(anywhere, list(matrices[: deck.reduce + 1])),
        narrow=(anywhere, matrices[deck.narrow]),
        later_attend=(anywhere, matrices[deck.later_attend]),
        later_merge=(anywhere, matrices[deck.later_merge]),
    )
    shapes = [blocks(matrix) for matrix in matrices[: deck.later_merge + 1]]
    outs = dict(input_grad=(vmem, shaped((rows, width))))
    outlets = dict(
        square=(2, *shapes[0]),
        tall=(2, depth // deck.chunks, *shapes[deck.reduce][1:]),
        narrow=(1, *shapes[deck.narrow]),
        attend=(1, *shapes[deck.later_attend]),
        merge=(1, *shapes[deck.later_merge]),
    )
    scratch, special = {}, {}
    if scatters:
        ready = [front.expand_grad, front.reduce_grad]
        ready = [grad.reshape(blocks(grad)) for grad in ready]
        tile = (*grid, 2 * SMALL, 256)
        outlets.update(small=(1, *tile))
        halves = [(s[3], s[4] // 2) for s in (*shapes, *(grad.shape for grad in ready), tile)]
        inputs.update(ready=(anywhere, ready))
        outs.update(
            shards=(vmem, [shaped((r // 2, 2 * h), F32) for r, h in halves]),
            staged=(anywhere, [shaped(s) for s in (*shapes, tile)]),
        )
        scratch.update(
            scatter_scratch(depth, parts, halves),
            early_grads=pltpu.VMEM((SMALL, width), F32),
            small_total=pltpu.VMEM((SMALL, model), F32),
        )
        special = dict(collective_id=1, has_side_effects=True)
    else:
        outs.update(
            staged=(anywhere, [shaped(s) for s in shapes]),
            early_grads=(vmem, shaped((SMALL, width), F32)),
            small_total=(vmem, shaped((SMALL, model), F32)),
        )
    scratch.update(
        encoded_grad=pltpu.VMEM((rows, width), F32),
        outlets={key: pltpu.VMEM(shape, BF16) for key, shape in outlets.items()},
        outlet_sems={key: pltpu.SemaphoreType.DMA((s[0],)) for key, s in outlets.items()},
    )
    sizes = dict(
        chips=chips, length=length, block=2 * (rows // chips), hidden_width=front.hidden.shape[1]
    )

    def body(at):
        at.fulls = list(at.staged)
        if scatters:
            at.fulls[deck.later_expand : deck.later_expand] = at.ready
        back_body(depth, parts, order, deck, owned, sizes, at)

    return call_kernel(body, inputs, outs, scratch, "back", 62, special)


def hand_over(sources, shapes, picks):
    def body(at):
        for target, pick in zip(at.targets, picks):
            pieces = [at.sources[k][rows, columns] for k, rows, columns in pick]
            value = pieces[0] if len(pieces) == 1 else jnp.concatenate(pieces, axis=1)
            target[...] = value.reshape(target.shape)

    inputs, outs = dict(sources=(VMEM, sources)), dict(targets=(VMEM, shapes))
    return call_kernel(body, inputs, outs, {}, "hand_over", 60, {}).targets


GATHER_PARTS = (
    (14, 0, 1, "zyx"),
    (0, 0, 1, "zxy"),
    (1, 0, 1, "zyx"),
    (2, 0, 1, "zxy"),
    (3, 0, 1, "xzy"),
    (4, 0, 1, "zyx"),
    (5, 0, 1, "zxy"),
    (6, 0, 1, "zyx"),
    (7, 0, 1, "zyx"),
    (8, 0, 4, "zyx"),
    (8, 1, 4, "xyz"),
    (8, 2, 4, "zyx"),
    (8, 3, 4, "yxz"),
    (9, 0, 1, "xzy"),
    (10, 0, 1, "yzx"),
    (11, 0, 1, "xzy"),
    (12, 0, 2, "xzy"),
    (12, 1, 2, "yxz"),
    (13, 0, 2, "yzx"),
    (13, 1, 2, "xzy"),
)

FRONT_ORDER = (
    16, 144, 72, 24, 32, 96, 8, 48, 104, 33, 112, 120, 17, 80, 128, 9, 73, 0, 81, 18, 152, 97, 19,
    25, 1, 10, 74, 26, 88, 11, 75, 40, 49, 2, 56, 89, 27, 145, 64, 3, 12, 4, 41, 90, 50, 20, 105,
    5, 42, 98, 57, 76, 28, 34, 91, 121, 35, 13, 65, 82, 122, 92, 43, 58, 21, 99, 66, 36, 6, 1000,
    22, 29, 59, 51, 100, 44, 83, 30, 14, 136, 77, 1001, 113, 1002, 93, 101, 1004, 67, 137, 106,
    60, 153, 1006, 84, 114, 37, 52, 1003, 102, 129, 45, 1005, 107, 68, 123, 154, 78, 85, 1007, 46,
    108, 38, 124, 115, 146, 53, 1008, 155, 86, 130, 94, 61, 1009, 116, 138, 147, 125, 54, 156, 69,
    1010, 126, 62, 131, 109, 1011, 148, 117, 70, 139, 132, 1012, 110, 157, 1013, 1014, 118, 1015,
    140, 1016, 149, 1017, 1018, 1019, 150, 1020, 141, 1021, 158, 1022, 1023, 142, 133, 1024, 1025,
    1026, 134, 1027, 1028,
)

SCATTER_PARTS = (
    (12, 0, 2, "yzx"),
    (12, 1, 2, "yzx"),
    (13, 0, 2, "yzx"),
    (13, 1, 2, "yzx"),
    (11, 0, 1, "yxz"),
    (10, 0, 1, "xzy"),
    (9, 0, 1, "xzy"),
    (4, 0, 1, "yxz"),
    (5, 0, 1, "xzy"),
    (6, 0, 1, "yzx"),
    (7, 0, 1, "yzx"),
    (8, 0, 4, "yzx"),
    (8, 1, 4, "xzy"),
    (8, 2, 4, "xyz"),
    (8, 3, 4, "yxz"),
    (3, 0, 1, "yxz"),
    (0, 0, 1, "xzy"),
    (1, 0, 1, "xyz"),
    (2, 0, 1, "yxz"),
    (14, 0, 1, "xzy"),
)

BACK_ORDER = (
    24, 1003, 0, 1002, 25, 1001, 1000, 8, 1, 16, 1004, 1006, 1008, 1005, 1009, 1007, 1010, 2,
    1011, 9, 1012, 17, 40, 32, 1013, 33, 41, 48, 56, 10, 1014, 64, 3, 26, 49, 57, 1015, 4, 72, 18,
    65, 11, 1016, 88, 73, 104, 50, 1017, 96, 27, 19, 42, 120, 51, 58, 66, 89, 80, 1018, 105, 74,
    1021, 121, 128, 43, 112, 97, 1019, 59, 1020, 106, 75, 90, 129, 52, 28, 81, 1022, 5, 113, 67,
    136, 98, 1023, 44, 122, 76, 137, 91, 144, 107, 152, 130, 12, 99, 108, 60, 145, 68, 34, 29,
    123, 100, 6, 82, 153, 77, 20, 114, 35, 69, 13, 131, 154, 124, 138, 146, 109, 36, 92, 155, 83,
    132, 53, 61, 115, 139, 54, 116, 110, 21, 147, 14, 133, 45, 70, 101, 156, 30, 125, 22, 140, 84,
    111, 93, 71, 78, 15, 148, 117, 157, 94, 85, 126, 37, 141, 7, 86, 134, 158, 46, 102, 62, 149,
    79, 31, 55, 118, 47, 87, 159, 38, 119, 142, 95, 23, 127, 63, 39, 135, 103, 150, 151, 143,
)


def cut_parts(parts, chip_rows):
    return [
        (k, chip_rows[k] // pieces * piece, chip_rows[k] // pieces, order)
        for k, piece, pieces, order in parts
    ]


def paths_fit(chip_rows):
    parts = GATHER_PARTS + SCATTER_PARTS
    whole = all(chip_rows[part[0]] % (16 * part[2]) == 0 for part in parts)
    return whole and lax.axis_size("seq") == 2 * SIDE and lax.axis_size("dp") == 4 * SIDE


def spread_rows(tiles, owned):
    tiles = tiles.astype(F32).reshape(-1, SMALL, 256)
    early = tiles[:, :2, : owned[0]].transpose(1, 0, 2).reshape(2, -1)
    later = tiles[:, 2:, : owned[1]].transpose(1, 0, 2).reshape(SMALL - 2, -1)
    early = jnp.pad(early, ((0, SMALL - 2), (0, 0)))
    return early, jnp.concatenate([later[:2], jnp.zeros_like(later[:2]), later[2:]], axis=0)


def collect_rows(early, later, owned):
    later = jnp.concatenate([later[:2], later[4:]], axis=0)
    tiles = [
        rows.reshape(rows.shape[0], -1, lanes).transpose(1, 0, 2)
        for rows, lanes in zip((early[:2], later), owned)
    ]
    tiles = [jnp.pad(t, ((0, 0), (0, 0), (0, 256 - t.shape[2]))) for t in tiles]
    return jnp.concatenate(tiles, axis=1).reshape(-1, 256)


def shards(
    encoder_input,
    visible_patches,
    sensor_index,
    encoder_gain,
    encoder_attend,
    encoder_merge,
    encoder_midnorm,
    encoder_expand,
    encoder_reduce,
    narrowing,
    placeholder,
    decoder_gain,
    decoder_attend,
    decoder_merge,
    decoder_midnorm,
    decoder_expand,
    decoder_reduce,
    cotangent,
):
    chips, length, width = encoder_input.shape
    model = cotangent.shape[2]
    axes, depth = ("dp", "seq"), 4
    deck = Deck(depth)
    devices = lax.axis_size("dp") * lax.axis_size("seq")
    owned = (width // devices, model // devices)
    x = encoder_input.reshape(chips * length, width)
    weights = (
        encoder_attend,
        encoder_merge,
        encoder_expand,
        encoder_reduce,
        narrowing,
        decoder_attend,
        decoder_merge,
        decoder_expand,
        decoder_reduce,
    )
    small = (encoder_gain, encoder_midnorm, decoder_gain, decoder_midnorm)
    data = (visible_patches, sensor_index, cotangent)
    chip_rows = [2 * w.shape[0] for w in weights]
    chip_rows = chip_rows[:1] * 3 + chip_rows[1:2] + chip_rows[2:3] * depth + chip_rows[3:] + [16]
    fits = paths_fit(chip_rows)
    if fits:
        weights += ((*small, placeholder),)
        parts = cut_parts(GATHER_PARTS, chip_rows)
        front = run_front(x, data, weights, depth, parts, FRONT_ORDER, deck, owned)
        matrices = [w.reshape(-1, w.shape[-1]) for w in front.wholes]
        data += (front.early_gains, front.later_small)
        parts = cut_parts(SCATTER_PARTS, chip_rows)
        back = run_back(front, x, data, matrices, depth, parts, BACK_ORDER, deck, owned)
        summed = back.shards
    else:
        rows = [jnp.pad(v, (0, 256 - v.shape[0]))[None, :] for v in small]
        rows.append(jnp.pad(placeholder, ((0, 0), (0, 256 - placeholder.shape[1]))))
        wholes = [
            lax.all_gather(w, axes, axis=0, tiled=True)
            for w in (*weights, jnp.concatenate(rows, axis=0))
        ]
        data += spread_rows(wholes[9], owned)
        front = run_front(x, data, wholes[:9], depth, None, (), deck, None)
        matrices = square_up(wholes[:9], deck)
        back = run_back(front, x, data, matrices, depth, None, (), deck, None)
        fulls = [full.reshape(-1, full.shape[-1]).astype(F32) for full in back.staged]
        fulls += [front.expand_grad.astype(F32), front.reduce_grad.astype(F32)]
        fulls.append(collect_rows(back.early_grads, back.small_total, owned))
        summed = [lax.psum_scatter(f, axes, scatter_dimension=0, tiled=True) for f in fulls]
    every = slice(None)
    third = width // 3
    picks = [[(k, every, slice(n * third, (n + 1) * third)) for n in range(3) for k in deck.attend]]
    picks.append([(deck.merge, every, every)])
    picks.append([(k, every, every) for k in deck.expand])
    picks += [[(k, every, every)] for k in range(deck.reduce, deck.small)]
    shapes = [shaped(w.shape, F32) for w in weights[:9]]
    for row, lanes in enumerate((owned[0], owned[0], owned[1], owned[1])):
        picks.append([(deck.small, slice(row, row + 1), slice(0, lanes))])
        shapes.append(shaped((1, lanes), F32))
    picks.append([(deck.small, slice(4, SMALL), slice(0, owned[1]))])
    shapes.append(shaped(placeholder.shape, F32))
    picks.append([(deck.count, every, every)])
    shapes.append(shaped(encoder_input.shape))
    sources = [*summed, back.input_grad]
    if fits:
        picks.append([(deck.count + 1, every, every)])
        shapes.append(shaped(cotangent.shape))
        sources.append(front.decoded.reshape(-1, model))
    given = hand_over(sources, shapes, picks)
    decoded = given[15] if fits else front.decoded
    gains = [gain.reshape(-1) for gain in given[9:13]]
    attend, merge, expand, reduce, narrow, later_attend, later_merge, *later = given[:9]
    return (
        decoded,
        given[14],
        gains[0],
        attend,
        merge,
        gains[1],
        expand,
        reduce,
        narrow,
        given[13],
        gains[2],
        later_attend,
        later_merge,
        gains[3],
        *later,
    )


def solution(mesh):
    placed = (
        P(("dp", "seq"), None, None),
        P(("dp", "seq"), None),
        P(("dp", "seq")),
        P(("dp", "seq")),
        P(("dp", "seq"), None),
        P(("dp", "seq"), None),
        P(("dp", "seq")),
        P(("dp", "seq"), None),
        P(("dp", "seq"), None),
        P(("dp", "seq"), None),
        P(None, ("dp", "seq")),
        P(("dp", "seq")),
        P(("dp", "seq"), None),
        P(("dp", "seq"), None),
        P(("dp", "seq")),
        P(("dp", "seq"), None),
        P(("dp", "seq"), None),
        P(("dp", "seq"), None, None),
    )
    return jax.shard_map(
        shards,
        mesh=mesh,
        in_specs=placed,
        out_specs=(
            P(("dp", "seq"), None, None),
            P(("dp", "seq"), None, None),
            P(("dp", "seq")),
            P(("dp", "seq"), None),
            P(("dp", "seq"), None),
            P(("dp", "seq")),
            P(("dp", "seq"), None),
            P(("dp", "seq"), None),
            P(("dp", "seq"), None),
            P(None, ("dp", "seq")),
            P(("dp", "seq")),
            P(("dp", "seq"), None),
            P(("dp", "seq"), None),
            P(("dp", "seq")),
            P(("dp", "seq"), None),
            P(("dp", "seq"), None),
        ),
        check_vma=False,
    )
```
